32 devices in a mesh: dp: 4 (over y, core), row: 2 (over x), col: 4 (over z).
Axes of the slice: x: 2, y: 2, z: 4, core: 2. Of those that a mesh axis runs over, the one named last changes fastest.
Arguments:
- inputs: bfloat16 [8192, 1024], P(('dp', 'col'), 'row'), may hold values from -6 to 6
- segments: int32 [16, 512], P('dp'), may hold values from 0 to 3, never falling along the last dimension, each value on 1 to 256 neighbouring positions
- cotangent: bfloat16 [8192, 1024], P(('dp', 'col'), 'row'), may hold values from -4 to 4
- w_query: float32 [1024, 2048], P(('row', 'dp'), 'col'), may hold values from -0.1875 to 0.1875
- keyvalue_weight: float32 [2, 1024, 1024], P(None, ('row', 'dp'), 'col'), may hold values from -0.1875 to 0.1875
- w_out: float32 [2048, 1024], P(('col', 'dp'), 'row'), may hold values from -0.5 to 0.5
- w_gate_up: float32 [2, 1024, 3072], P(None, ('row', 'dp'), 'col'), may hold values from -0.1875 to 0.1875
- w_down: float32 [3072, 1024], P(('col', 'dp'), 'row'), may hold values from -0.109375 to 0.109375
- first_query: float32 [1024, 2048], P(('row', 'dp'), 'col'), may hold values from -59.73638 to 59.73638
- keyvalue_first_moment: float32 [2, 1024, 1024], P(None, ('row', 'dp'), 'col'), may hold values from -59.73638 to 59.73638
- first_out: float32 [2048, 1024], P(('col', 'dp'), 'row'), may hold values from -14.934095 to 14.934095
- first_gate_up: float32 [2, 1024, 3072], P(None, ('row', 'dp'), 'col'), may hold values from -20.907734 to 20.907734
- first_down: float32 [3072, 1024], P(('col', 'dp'), 'row'), may hold values from -35.841827 to 35.841827
- second_query: float32 [1024, 2048], P(('row', 'dp'), 'col'), may hold values from 8.192 to 32.768
- keyvalue_second_moment: float32 [2, 1024, 1024], P(None, ('row', 'dp'), 'col'), may hold values from 8.192 to 32.768
- second_out: float32 [2048, 1024], P(('col', 'dp'), 'row'), may hold values from 0.512 to 2.048
- second_gate_up: float32 [2, 1024, 3072], P(None, ('row', 'dp'), 'col'), may hold values from 1.00352 to 4.01408
- second_down: float32 [3072, 1024], P(('col', 'dp'), 'row'), may hold values from 2.94912 to 11.79648
- norm_gains: float32 [2304], replicated, may hold values from 0.4 to 2.4
- gains_first: float32 [2304], replicated, may hold values from -119.47276 to 119.47276
- gains_second: float32 [2304], replicated, may hold values from 32.768 to 131.072
Outputs:
- outputs: float32 [8192, 1024], P(('dp', 'col'), 'row')
- input_grad: float32 [8192, 1024], P(('dp', 'col'), 'row')
- new_query: float32 [1024, 2048], P(('row', 'dp'), 'col')
- new_keyval: float32 [2, 1024, 1024], P(None, ('row', 'dp'), 'col')
- new_out: float32 [2048, 1024], P(('col', 'dp'), 'row')
- new_gate_up: float32 [2, 1024, 3072], P(None, ('row', 'dp'), 'col')
- new_down: float32 [3072, 1024], P(('col', 'dp'), 'row')
- new_first_query: float32 [1024, 2048], P(('row', 'dp'), 'col')
- new_first_keyval: float32 [2, 1024, 1024], P(None, ('row', 'dp'), 'col')
- new_first_out: float32 [2048, 1024], P(('col', 'dp'), 'row')
- new_first_gate_up: float32 [2, 1024, 3072], P(None, ('row', 'dp'), 'col')
- new_first_down: float32 [3072, 1024], P(('col', 'dp'), 'row')
- new_second_query: float32 [1024, 2048], P(('row', 'dp'), 'col')
- new_second_keyval: float32 [2, 1024, 1024], P(None, ('row', 'dp'), 'col')
- new_second_out: float32 [2048, 1024], P(('col', 'dp'), 'row')
- new_second_gate_up: float32 [2, 1024, 3072], P(None, ('row', 'dp'), 'col')
- new_second_down: float32 [3072, 1024], P(('col', 'dp'), 'row')
- new_gains: float32 [2304], replicated
- new_gains_first: float32 [2304], replicated
- new_gains_second: float32 [2304], replicated
The draws below stay inside these ranges and needn't reach their ends.
All inputs are finite; a program needn't handle non-finite values.
Results may differ from the reference program's by a relative error of at most 0.014.
The reference program's roundings to bfloat16 on the way count: a program that leaves them out, or rounds other values in their place, can miss the bound.
Values may be sent and summed in bfloat16 or wider, within the bound.
A program may use at most 128 MiB of HBM per device.

```python
import math
import jax
import jax.numpy as jnp
import numpy as np
from jax import lax

MODEL_WIDTH = 1024
QUERY_HEAD_COUNT = 16
KEYVALUE_HEADS = 8
HEAD_SIZE = 128
FF = 3072
SEQUENCE_LENGTH = 512
SEQ_DP = 4
SEG_COUNT = 4
SEG_MOST = 256
STEP = 10
SEQS = 16
TOKEN_TOTAL = 8192
N_DP = 4


def draw_inputs(key, part):
    key = jax.random.fold_in(key, 5)
    column_scale = 0.5 + jnp.arange(MODEL_WIDTH, dtype=jnp.float32) / MODEL_WIDTH
    values = jnp.clip(jax.random.normal(key, (TOKEN_TOTAL, MODEL_WIDTH), jnp.float32), -4.0, 4.0) * column_scale
    return values.astype(jnp.bfloat16)


def draw_norm_gains(key, part):
    key = jax.random.fold_in(key, 7)
    key_attn, key_mlp, key_heads = jax.random.split(key, 3)
    position = jnp.arange(MODEL_WIDTH, dtype=jnp.float32) / MODEL_WIDTH
    column_ramp = 0.6 + position
    noise_attn = jnp.exp(jax.random.uniform(key_attn, (MODEL_WIDTH,), jnp.float32, -0.2, 0.2))
    noise_mlp = jnp.exp(jax.random.uniform(key_mlp, (MODEL_WIDTH,), jnp.float32, -0.2, 0.2))
    head_gains = jnp.exp(jax.random.uniform(key_heads, (2 * HEAD_SIZE,), jnp.float32, 0.0, 0.69))
    return jnp.concatenate([column_ramp * noise_attn, column_ramp * noise_mlp, head_gains]).astype(jnp.float32)


def level_of(rng, shape, shards, low, largest):
    gain, own = 1.0, jax.random.fold_in(rng, 6)
    for axis_at, shards_of in shards:
        heights = jnp.exp(jax.random.uniform(jax.random.fold_in(own, axis_at), (shards_of,), jnp.float32, low / len(shards), largest / len(shards)))
        gain = gain * jnp.repeat(heights, shape[axis_at] // shards_of).reshape([-1 if axis == axis_at else 1 for axis in range(len(shape))])
    return gain


def split_up(number_of, total, limit, slope):
    portions = [(1 << 20) // math.isqrt(standing ** slope) + 1 for standing in range(2, number_of + 1)]
    spare, given = total - limit - (number_of - 1), [1] * (number_of - 1)
    while spare > 0:
        movable = [i for i in range(number_of - 1) if given[i] < limit]
        whole, left = sum([portions[i] for i in movable]), spare
        for i in movable:
            more = min(limit - given[i], max(1, left * portions[i] // whole), spare)
            given[i] = given[i] + more
            spare = spare - more
    return np.array([limit] + given)


def ragged(stream_key, count, total, bound, lean):
    if count == 2:
        one = jax.random.randint(stream_key, (), max(1, total - bound), min(bound, total - 1) + 1)
        return jnp.stack([one, total - one])
    tallies = jnp.asarray(split_up(count, total, bound, lean), jnp.int32)
    twos = (count - 1) // 2
    giver, receiver = tallies[1:1 + 2 * twos:2], tallies[2:2 + 2 * twos:2]
    slack = jnp.minimum(giver - 1, bound - receiver)
    moved = jax.random.randint(jax.random.fold_in(stream_key, 1), (twos,), 0, 1 << 20) % (slack + 1)
    tallies = tallies.at[1:1 + 2 * twos:2].set(giver - moved).at[2:2 + 2 * twos:2].set(receiver + moved)
    return tallies[jax.random.permutation(jax.random.fold_in(stream_key, 2), count)]


def gaussian(rng, extent, deviation, most, pieces=(), held_as=jnp.bfloat16):
    values = jax.random.normal(rng, extent, jnp.float32) * deviation
    if len(pieces) > 0:
        values = level_of(rng, extent, pieces, -0.22, 0.18) * values
    return jnp.clip(values, min=-most, max=most).astype(held_as)


def setup_inputs(seed: int = 0) -> dict:
    key_of = jax.random.split(jax.random.key(seed), 22)
    inputs = draw_inputs(jax.random.fold_in(key_of[21], 71), 0)
    segments = jax.vmap(lambda own: jnp.searchsorted(jnp.cumsum(ragged(own, SEG_COUNT, SEQUENCE_LENGTH, SEG_MOST, 1)), jnp.arange(SEQUENCE_LENGTH), side="right"))(jax.random.split(key_of[1], SEQS)).reshape((SEQS, SEQUENCE_LENGTH)).astype(jnp.int32)
    cotangent = gaussian(key_of[2], (TOKEN_TOTAL, MODEL_WIDTH), 1.0, 4.0, ((0, 16), (1, 2)))
    w_query = gaussian(key_of[3], (MODEL_WIDTH, QUERY_HEAD_COUNT * HEAD_SIZE), MODEL_WIDTH ** -0.5, 0.1875, ((0, 8), (1, 4)), jnp.float32)
    keyvalue_weight = gaussian(key_of[4], (2, MODEL_WIDTH, KEYVALUE_HEADS * HEAD_SIZE), MODEL_WIDTH ** -0.5, 0.1875, ((1, 8), (2, 4)), jnp.float32)
    w_out = gaussian(key_of[5], (QUERY_HEAD_COUNT * HEAD_SIZE, MODEL_WIDTH), (QUERY_HEAD_COUNT * HEAD_SIZE // 16) ** -0.5, 0.5, ((0, 16), (1, 2)), jnp.float32)
    w_gate_up = gaussian(key_of[6], (2, MODEL_WIDTH, FF), MODEL_WIDTH ** -0.5, 0.1875, ((1, 8), (2, 4)), jnp.float32)
    w_down = gaussian(key_of[7], (FF, MODEL_WIDTH), FF ** -0.5, 0.109375, ((0, 16), (1, 2)), jnp.float32)
    first_query = gaussian(key_of[8], (MODEL_WIDTH, QUERY_HEAD_COUNT * HEAD_SIZE), (0.11 * TOKEN_TOTAL ** 0.5), 59.73638, ((0, 8), (1, 4)), jnp.float32)
    keyvalue_first_moment = gaussian(key_of[9], (2, MODEL_WIDTH, KEYVALUE_HEADS * HEAD_SIZE), (0.11 * TOKEN_TOTAL ** 0.5), 59.73638, ((1, 8), (2, 4)), jnp.float32)
    first_out = gaussian(key_of[10], (QUERY_HEAD_COUNT * HEAD_SIZE, MODEL_WIDTH), (0.0275 * TOKEN_TOTAL ** 0.5), 14.934095, ((0, 16), (1, 2)), jnp.float32)
    first_gate_up = gaussian(key_of[11], (2, MODEL_WIDTH, FF), (0.0385 * TOKEN_TOTAL ** 0.5), 20.907734, ((1, 8), (2, 4)), jnp.float32)
    first_down = gaussian(key_of[12], (FF, MODEL_WIDTH), (0.066 * TOKEN_TOTAL ** 0.5), 35.841827, ((0, 16), (1, 2)), jnp.float32)
    second_query = jnp.clip(jnp.exp(math.log(32.768) - 1.3862944 * jax.random.uniform(key_of[13], (MODEL_WIDTH, QUERY_HEAD_COUNT * HEAD_SIZE), jnp.float32) ** level_of(key_of[13], (MODEL_WIDTH, QUERY_HEAD_COUNT * HEAD_SIZE), ((0, 8), (1, 4)), -0.2, 0.2)), 8.192, 32.768)
    keyvalue_second_moment = jnp.clip(jnp.exp(math.log(32.768) - 1.3862944 * jax.random.uniform(key_of[14], (2, MODEL_WIDTH, KEYVALUE_HEADS * HEAD_SIZE), jnp.float32) ** level_of(key_of[14], (2, MODEL_WIDTH, KEYVALUE_HEADS * HEAD_SIZE), ((1, 8), (2, 4)), -0.2, 0.2)), 8.192, 32.768)
    second_out = jnp.clip(jnp.exp(math.log(2.048) - 1.3862944 * jax.random.uniform(key_of[15], (QUERY_HEAD_COUNT * HEAD_SIZE, MODEL_WIDTH), jnp.float32) ** level_of(key_of[15], (QUERY_HEAD_COUNT * HEAD_SIZE, MODEL_WIDTH), ((0, 16), (1, 2)), -0.2, 0.2)), 0.512, 2.048)
    second_gate_up = jnp.clip(jnp.exp(math.log(4.01408) - 1.3862944 * jax.random.uniform(key_of[16], (2, MODEL_WIDTH, FF), jnp.float32) ** level_of(key_of[16], (2, MODEL_WIDTH, FF), ((1, 8), (2, 4)), -0.2, 0.2)), 1.00352, 4.01408)
    second_down = jnp.clip(jnp.exp(math.log(11.79648) - 1.3862944 * jax.random.uniform(key_of[17], (FF, MODEL_WIDTH), jnp.float32) ** level_of(key_of[17], (FF, MODEL_WIDTH), ((0, 16), (1, 2)), -0.2, 0.2)), 2.94912, 11.79648)
    norm_gains = draw_norm_gains(jax.random.fold_in(key_of[21], 71), 0)
    gains_first = gaussian(key_of[19], (2 * MODEL_WIDTH + 2 * HEAD_SIZE,), (0.22 * TOKEN_TOTAL ** 0.5), 119.47276, (), jnp.float32)
    gains_second = jnp.clip(jnp.exp(jax.random.uniform(key_of[20], (2 * MODEL_WIDTH + 2 * HEAD_SIZE,), jnp.float32, math.log(32.768), math.log(131.072))), 32.768, 131.072)
    return {"inputs": inputs, "segments": segments, "cotangent": cotangent, "w_query": w_query, "keyvalue_weight": keyvalue_weight, "w_out": w_out, "w_gate_up": w_gate_up, "w_down": w_down, "first_query": first_query, "keyvalue_first_moment": keyvalue_first_moment, "first_out": first_out, "first_gate_up": first_gate_up, "first_down": first_down, "second_query": second_query, "keyvalue_second_moment": keyvalue_second_moment, "second_out": second_out, "second_gate_up": second_gate_up, "second_down": second_down, "norm_gains": norm_gains, "gains_first": gains_first, "gains_second": gains_second}


@jax.custom_vjp
def reduced_precision(v):
    return lax.optimization_barrier(v.astype(jnp.bfloat16)).astype(jnp.float32)

@jax.custom_vjp
def low_back(v):
    return v

def low_keep(v):
    return (reduced_precision(v), None)

def low_pass(kept, grad):
    return (grad,)

def back_keep(v):
    return (v, None)

def back_low(kept, grad):
    return (reduced_precision(grad),)
reduced_precision.defvjp(low_keep, low_pass)
low_back.defvjp(back_keep, back_low)
epsilon = 1e-06
rope_base = 1000000.0
masked_score = -1e+30
highest = lax.Precision.HIGHEST
beta_first = 0.9
beta_second = 0.999
learning_rate = 0.05
gains_rate = 0.6
adam_epsilon = 1e-08
weight_decay = 0.1

def rms_scale(values):
    return lax.rsqrt(lax.optimization_barrier(jnp.mean(values * values, axis=-1, keepdims=True)) + epsilon)

def norm_apply(values, gain_vec):
    return values * rms_scale(values) * gain_vec

def rotate(values, cosine_table, sinus_table):
    half_width = values.shape[-1] // 2
    turned = jnp.concatenate([-values[..., half_width:], values[..., :half_width]], axis=-1)
    return values * cosine_table + turned * sinus_table

def rope_tables(positions):
    exponent = jnp.arange(HEAD_SIZE // 2, dtype=jnp.float32) * (2.0 / HEAD_SIZE)
    inverse = jnp.exp(-jnp.log(jnp.float32(rope_base)) * exponent)
    angles = positions.astype(jnp.float32)[..., None] * inverse
    angles = jnp.concatenate([angles, angles], axis=-1)
    return (jnp.cos(angles), jnp.sin(angles))

def allowed(segment_ids):
    length = segment_ids.shape[-1]
    order = jnp.arange(length)
    causal = order[None, :] <= order[:, None]
    return (segment_ids[..., :, None] == segment_ids[..., None, :]) & causal

def head_slice_part(pre_values, gain_vec, cosine_table, sinus_table):
    return rotate(norm_apply(pre_values, gain_vec), cosine_table, sinus_table)

def attend_single(item_set):
    query_matrix, keys_in, values_in, permitted_mask = item_set
    length = query_matrix.shape[0]
    grouped = query_matrix.reshape(length, keys_in.shape[1], -1, HEAD_SIZE)
    scores = low_back(jnp.einsum('qhgd,khd->hgqk', grouped, keys_in, precision=highest) * HEAD_SIZE ** (-0.5))
    scores = jnp.where(permitted_mask, scores, masked_score)
    probs = reduced_precision(jax.nn.softmax(scores, axis=-1))
    blended_output = jnp.einsum('hgqk,khd->qhgd', probs, values_in, precision=highest)
    return blended_output.reshape(length, -1)

def block_forward(resid_in, segment_ids, w_query, keyvalue_weight, w_out, w_gate_up, w_down, norm_gains):
    local_token_count = resid_in.shape[0]
    packed_sequence_list = segment_ids.shape[0]
    gain_attn = norm_gains[:MODEL_WIDTH]
    gain_mlp = norm_gains[MODEL_WIDTH:2 * MODEL_WIDTH]
    gain_query = norm_gains[2 * MODEL_WIDTH:2 * MODEL_WIDTH + HEAD_SIZE]
    key_norm_gain = norm_gains[2 * MODEL_WIDTH + HEAD_SIZE:]
    permitted_mask = allowed(segment_ids)
    positions = lax.optimization_barrier(jnp.sum(permitted_mask.astype(jnp.int32), axis=-1)) - 1
    cosine_table, sinus_table = rope_tables(positions.reshape(-1))
    cosine_table = cosine_table[:, None, :]
    sinus_table = sinus_table[:, None, :]
    normed_attn = reduced_precision(norm_apply(resid_in, gain_attn))
    query_pre = low_back(jnp.dot(normed_attn, reduced_precision(w_query), precision=highest))
    keyvalue_preactivation = low_back(jnp.einsum('td,sdf->stf', normed_attn, reduced_precision(keyvalue_weight), precision=highest))
    query_matrix = reduced_precision(head_slice_part(query_pre.reshape(local_token_count, QUERY_HEAD_COUNT, HEAD_SIZE), gain_query, cosine_table, sinus_table))
    every_key_row = reduced_precision(head_slice_part(keyvalue_preactivation[0].reshape(local_token_count, KEYVALUE_HEADS, HEAD_SIZE), key_norm_gain, cosine_table, sinus_table))
    every_value_row = reduced_precision(keyvalue_preactivation[1].reshape(local_token_count, KEYVALUE_HEADS, HEAD_SIZE))
    blended_output = lax.map(jax.checkpoint(attend_single), (query_matrix.reshape(packed_sequence_list, SEQUENCE_LENGTH, QUERY_HEAD_COUNT, HEAD_SIZE), every_key_row.reshape(packed_sequence_list, SEQUENCE_LENGTH, KEYVALUE_HEADS, HEAD_SIZE), every_value_row.reshape(packed_sequence_list, SEQUENCE_LENGTH, KEYVALUE_HEADS, HEAD_SIZE), permitted_mask))
    attn_values = reduced_precision(low_back(blended_output.reshape(local_token_count, QUERY_HEAD_COUNT * HEAD_SIZE)))
    resid_mid = resid_in + low_back(jnp.dot(attn_values, reduced_precision(w_out), precision=highest))
    normed_mlp = reduced_precision(norm_apply(resid_mid, gain_mlp))
    gate_up = low_back(jnp.einsum('td,sdf->stf', normed_mlp, reduced_precision(w_gate_up), precision=highest))
    hidden = reduced_precision(jax.nn.silu(gate_up[0]) * gate_up[1])
    return resid_mid + low_back(jnp.dot(hidden, reduced_precision(w_down), precision=highest))

def adam_update(weight, gradient, first, second, decay, rate):
    first_new = beta_first * first + (1.0 - beta_first) * gradient
    second_new = beta_second * second + (1.0 - beta_second) * gradient * gradient
    first_hat = first_new / (1.0 - beta_first ** STEP)
    second_hat = second_new / (1.0 - beta_second ** STEP)
    weight_new = weight - rate * (first_hat / (jnp.sqrt(second_hat) + adam_epsilon) + decay * weight)
    return (weight_new, first_new, second_new)

def reference(inputs, segments, cotangent, w_query, keyvalue_weight, w_out, w_gate_up, w_down, first_query, keyvalue_first_moment, first_out, first_gate_up, first_down, second_query, keyvalue_second_moment, second_out, second_gate_up, second_down, norm_gains, gains_first, gains_second):
    weights = (w_query, keyvalue_weight, w_out, w_gate_up, w_down, norm_gains)
    group_tokens = SEQ_DP * SEQUENCE_LENGTH
    resid_groups = inputs.astype(jnp.float32).reshape(N_DP, group_tokens, MODEL_WIDTH)
    grad_groups = cotangent.astype(jnp.float32).reshape(N_DP, group_tokens, MODEL_WIDTH)
    segment_groups = segments.reshape(N_DP, SEQ_DP, SEQUENCE_LENGTH)

    def one_group(totals, item_set):
        resid_group, segment_group, grad_group = item_set

        def forward(resid_val, *params):
            return block_forward(resid_val, segment_group, *params)
        outputs_group, pullback = jax.vjp(forward, resid_group, *weights)
        gradients = pullback(grad_group)
        summed = tuple((running + fresh for running, fresh in zip(totals, gradients[1:])))
        return (summed, (outputs_group, gradients[0]))
    starts = tuple((jnp.zeros_like(weight) for weight in weights))
    totals, (outputs_all, input_grads) = lax.scan(one_group, starts, (resid_groups, segment_groups, grad_groups))
    query_new = adam_update(w_query, totals[0], first_query, second_query, weight_decay, learning_rate)
    keyval_new = adam_update(keyvalue_weight, totals[1], keyvalue_first_moment, keyvalue_second_moment, weight_decay, learning_rate)
    out_new = adam_update(w_out, totals[2], first_out, second_out, weight_decay, learning_rate)
    gate_up_new = adam_update(w_gate_up, totals[3], first_gate_up, second_gate_up, weight_decay, learning_rate)
    down_new = adam_update(w_down, totals[4], first_down, second_down, weight_decay, learning_rate)
    gains_new = adam_update(norm_gains, totals[5], gains_first, gains_second, 0.0, gains_rate)
    return (outputs_all.reshape(TOKEN_TOTAL, MODEL_WIDTH), input_grads.reshape(TOKEN_TOTAL, MODEL_WIDTH), query_new[0], keyval_new[0], out_new[0], gate_up_new[0], down_new[0], query_new[1], keyval_new[1], out_new[1], gate_up_new[1], down_new[1], query_new[2], keyval_new[2], out_new[2], gate_up_new[2], down_new[2], gains_new[0], gains_new[1], gains_new[2])
```

```python
import jax
import jax.numpy as jnp
from jax import lax
from jax.experimental import pallas as pl
from jax.experimental.pallas import tpu as pltpu
from jax.sharding import PartitionSpec as P

MODEL_WIDTH = 1024
HEAD_SIZE = 128
STEP = 10


epsilon = 1e-06
rope_base = 1000000.0
masked_score = -1e30
beta_first = 0.9
beta_second = 0.999
learning_rate = 0.05
gains_rate = 0.6
adam_epsilon = 1e-08
weight_decay = 0.1
score_scale = HEAD_SIZE ** (-0.5)


def rms_scale(values):
    return lax.rsqrt(jnp.mean(values * values, axis=-1, keepdims=True) + epsilon)


def rotate(values, cosine_table, sinus_table):
    half_width = values.shape[-1] // 2
    turned = jnp.concatenate([-values[..., half_width:], values[..., :half_width]], axis=-1)
    return values * cosine_table + turned * sinus_table


def rope_tables(positions):
    exponent = jnp.arange(HEAD_SIZE // 2, dtype=jnp.float32) * (2.0 / HEAD_SIZE)
    inverse = jnp.exp(-jnp.log(jnp.float32(rope_base)) * exponent)
    angles = positions.astype(jnp.float32)[..., None] * inverse
    angles = jnp.concatenate([angles, angles], axis=-1)
    return (jnp.cos(angles), jnp.sin(angles))


def allowed(segment_ids):
    length = segment_ids.shape[-1]
    order = jnp.arange(length)
    causal = order[None, :] <= order[:, None]
    return (segment_ids[..., :, None] == segment_ids[..., None, :]) & causal


def head_slice_part(pre_values, gain_vec, cosine_table, sinus_table):
    return rotate(pre_values * rms_scale(pre_values) * gain_vec, cosine_table, sinus_table)


def swap_row(values):
    return lax.ppermute(values, "row", [(0, 1), (1, 0)])


def own_half(values, axis, row_index):
    width = values.shape[axis] // 2
    return lax.dynamic_slice_in_dim(values, row_index * width, width, axis)


def other_half(values, axis, row_index):
    width = values.shape[axis] // 2
    return lax.dynamic_slice_in_dim(values, (1 - row_index) * width, width, axis)


def in_row_order(own, peer, row_index, axis):
    return jnp.where(
        row_index == 0,
        jnp.concatenate([own, peer], axis=axis),
        jnp.concatenate([peer, own], axis=axis),
    )


def exchange_columns(block, row_index):
    peer = swap_row(other_half(block, 1, row_index))
    return in_row_order(own_half(block, 1, row_index)[None], peer[None], row_index, 0)


def return_columns(pieces, row_index):
    own = lax.dynamic_index_in_dim(pieces, row_index, 0, keepdims=False)
    peer = swap_row(lax.dynamic_index_in_dim(pieces, 1 - row_index, 0, keepdims=False))
    return in_row_order(own, peer, row_index, 1)


def block_moves(dp_count):
    half = dp_count // 2
    moves = []
    for row in range(2):
        for place in range(dp_count):
            target = 2 * (2 * (place % half) + row) + place // half
            moves.append((2 * place + row, target))
    return moves


def gather_in(pieces):
    dp_count, col_count = lax.axis_size("dp"), lax.axis_size("col")
    gathered = lax.all_gather(pieces, ("dp", "col"), axis=0, tiled=False)
    rows, columns = pieces.shape[1:]
    gathered = gathered.reshape(dp_count, col_count, 2, rows, columns)
    return gathered.transpose(2, 0, 3, 1, 4).reshape(2 * dp_count * rows, col_count * columns)


def scatter_in(grad):
    dp_count, col_count = lax.axis_size("dp"), lax.axis_size("col")
    rows, columns = grad.shape[0] // (2 * dp_count), grad.shape[1] // col_count
    pieces = grad.reshape(2, dp_count, rows, col_count, columns).transpose(1, 3, 0, 2, 4)
    pieces = pieces.reshape(dp_count * col_count, 2, rows, columns)
    return lax.psum_scatter(pieces, ("dp", "col"), scatter_dimension=0, tiled=False)


def gather_out(shard):
    dp_count, col_count = lax.axis_size("dp"), lax.axis_size("col")
    moved = lax.ppermute(shard, ("dp", "row"), block_moves(dp_count))
    gathered = lax.all_gather(moved, ("dp", "col"), axis=0, tiled=False)
    rows, columns = shard.shape
    gathered = gathered.reshape(dp_count // 2, 2, col_count, rows, columns)
    return gathered.transpose(2, 0, 3, 1, 4).reshape(
        col_count * (dp_count // 2) * rows, 2 * columns
    )


def scatter_out(grad):
    dp_count, col_count = lax.axis_size("dp"), lax.axis_size("col")
    rows, columns = grad.shape[0] // (col_count * (dp_count // 2)), grad.shape[1] // 2
    pieces = grad.reshape(col_count, dp_count // 2, rows, 2, columns).transpose(1, 3, 0, 2, 4)
    pieces = pieces.reshape(dp_count * col_count, rows, columns)
    own = lax.psum_scatter(pieces, ("dp", "col"), scatter_dimension=0, tiled=False)
    back = [(target, source) for source, target in block_moves(dp_count)]
    return lax.ppermute(own, ("dp", "row"), back)


def dot(left, right, contract):
    return lax.dot_general(
        left, right, ((contract[0], contract[1]), ((), ())), preferred_element_type=jnp.float32
    )


def probabilities(query, keys, permitted):
    scores = dot(query, keys, ((1,), (1,))) * score_scale
    scores = jnp.where(permitted, scores, masked_score)
    exp_scores = jnp.exp(scores - jnp.max(scores, axis=-1, keepdims=True))
    return exp_scores / jnp.sum(exp_scores, axis=-1, keepdims=True)


def permitted_of(seg_column, seg_line):
    length = seg_line.shape[1]
    place = lax.broadcasted_iota(jnp.int32, (length, length), 0)
    other = lax.broadcasted_iota(jnp.int32, (length, length), 1)
    return (seg_column[...] == seg_line[...]) & (other <= place)


def attend_forward_kernel(seg_column, seg_line, query, keys, values, mixed):
    permitted = permitted_of(seg_column, seg_line)
    for head in range(query.shape[1] // HEAD_SIZE):
        columns = slice(head * HEAD_SIZE, (head + 1) * HEAD_SIZE)
        probs = probabilities(query[:, columns], keys[...], permitted)
        mixed[:, columns] = dot(
            probs.astype(jnp.bfloat16), values[...], ((1,), (0,))
        ).astype(jnp.bfloat16)


def attend_backward_kernel(
    seg_column, seg_line, query, keys, values, grad, query_grad, key_grad, value_grad
):
    permitted = permitted_of(seg_column, seg_line)
    key_total, value_total = None, None
    for head in range(query.shape[1] // HEAD_SIZE):
        columns = slice(head * HEAD_SIZE, (head + 1) * HEAD_SIZE)
        probs = probabilities(query[:, columns], keys[...], permitted)
        prob_grad = dot(grad[:, columns], values[...], ((1,), (1,)))
        inner = jnp.sum(probs * prob_grad, axis=-1, keepdims=True)
        score_low = (probs * (prob_grad - inner)).astype(jnp.bfloat16)
        query_grad[:, columns] = dot(score_low, keys[...], ((1,), (0,))) * score_scale
        key_part = dot(score_low, query[:, columns], ((0,), (0,)))
        value_part = dot(probs.astype(jnp.bfloat16), grad[:, columns], ((0,), (0,)))
        key_total = key_part if head == 0 else key_total + key_part
        value_total = value_part if head == 0 else value_total + value_part
    key_grad[...] = key_total * score_scale
    value_grad[...] = value_total


def attention_call(kernel, seg_column, seg_line, arrays, outs, kv_count):
    length = seg_column.shape[0]

    def block(array):
        return pl.BlockSpec((length, array.shape[1] // kv_count), lambda head: (0, head))

    return pl.pallas_call(
        kernel,
        grid=(kv_count,),
        in_specs=[
            pl.BlockSpec(seg_column.shape, lambda head: (0, 0)),
            pl.BlockSpec(seg_line.shape, lambda head: (0, 0)),
        ]
        + [block(array) for array in arrays],
        out_specs=[block(out) for out in outs],
        out_shape=list(outs),
        compiler_params=pltpu.CompilerParams(vmem_limit_bytes=48 * 1024 * 1024),
    )(seg_column, seg_line, *arrays)


def norm_back(grad_normed, resid, scale, gain_vec):
    weighted = grad_normed * gain_vec
    inner = jnp.sum(weighted * resid, axis=-1, keepdims=True)
    resid_grad = scale * weighted - resid * (scale * scale * scale) * inner / MODEL_WIDTH
    return resid_grad


def adam_update(weight, gradient, first, second, decay, rate):
    first_new = beta_first * first + (1.0 - beta_first) * gradient
    second_new = beta_second * second + (1.0 - beta_second) * gradient * gradient
    first_hat = first_new / (1.0 - beta_first**STEP)
    second_hat = second_new / (1.0 - beta_second**STEP)
    weight_new = weight - rate * (
        first_hat / (jnp.sqrt(second_hat) + adam_epsilon) + decay * weight
    )
    return (weight_new, first_new, second_new)


def shards(
    inputs,
    segments,
    cotangent,
    w_query,
    keyvalue_weight,
    w_out,
    w_gate_up,
    w_down,
    first_query,
    keyvalue_first_moment,
    first_out,
    first_gate_up,
    first_down,
    second_query,
    keyvalue_second_moment,
    second_out,
    second_gate_up,
    second_down,
    norm_gains,
    gains_first,
    gains_second,
):
    low = jnp.bfloat16
    row_index = lax.axis_index("row")
    tokens = inputs.shape[0]
    width_row = inputs.shape[1]

    query_key_value = jnp.concatenate(
        [
            exchange_columns(block.astype(low), row_index)
            for block in (w_query, keyvalue_weight[0], keyvalue_weight[1])
        ],
        axis=2,
    )
    in_block = gather_in(query_key_value)
    out_block = gather_out(w_out.astype(low))
    gate_up_block = gather_in(
        jnp.concatenate(
            [exchange_columns(w_gate_up[which].astype(low), row_index) for which in (0, 1)],
            axis=2,
        )
    )
    down_block = gather_out(w_down.astype(low))

    gain_attn = norm_gains[:MODEL_WIDTH]
    gain_mlp = norm_gains[MODEL_WIDTH : 2 * MODEL_WIDTH]
    gain_query = norm_gains[2 * MODEL_WIDTH : 2 * MODEL_WIDTH + HEAD_SIZE]
    key_norm_gain = norm_gains[2 * MODEL_WIDTH + HEAD_SIZE :]
    segment = lax.dynamic_index_in_dim(segments, lax.axis_index("col"), 0, keepdims=False)
    seg_column, seg_line = segment[:, None], segment[None, :]
    positions = jnp.sum(allowed(segment).astype(jnp.int32), axis=-1) - 1
    cosine_table, sinus_table = rope_tables(positions)
    cosine_table = cosine_table[:, None, :]
    sinus_table = sinus_table[:, None, :]

    resid_in = in_row_order(inputs, swap_row(inputs), row_index, 1).astype(jnp.float32)
    scale_attn = rms_scale(resid_in)
    normed_attn = (resid_in * scale_attn * gain_attn).astype(low)
    col_count = lax.axis_size("col")
    query_wide = w_query.shape[1] // 2
    key_wide = keyvalue_weight.shape[2] // 2
    projected = dot(normed_attn, in_block, ((1,), (0,))).reshape(tokens, col_count, -1)
    query_heads = projected[:, :, :query_wide].reshape(tokens, -1, HEAD_SIZE)
    key_heads = projected[:, :, query_wide : query_wide + key_wide].reshape(tokens, -1, HEAD_SIZE)
    value_low = projected[:, :, query_wide + key_wide :].reshape(tokens, -1).astype(low)
    kv_count = key_heads.shape[1]

    def normed_heads(pre_values, gain_vec):
        return head_slice_part(pre_values, gain_vec, cosine_table, sinus_table)

    query_rot, pull_query = jax.vjp(normed_heads, query_heads, gain_query)
    key_rot, pull_key = jax.vjp(normed_heads, key_heads, key_norm_gain)
    query_low = query_rot.astype(low).reshape(tokens, -1)
    key_low = key_rot.astype(low).reshape(tokens, -1)
    (attn_low,) = attention_call(
        attend_forward_kernel,
        seg_column,
        seg_line,
        (query_low, key_low, value_low),
        (jax.ShapeDtypeStruct(query_low.shape, low),),
        kv_count,
    )
    attn_part = dot(attn_low, out_block, ((1,), (0,))).astype(low)
    attn_sum = attn_part.astype(jnp.float32) + swap_row(attn_part).astype(jnp.float32)
    resid_mid = resid_in + attn_sum
    scale_mlp = rms_scale(resid_mid)
    normed_mlp = (resid_mid * scale_mlp * gain_mlp).astype(low)
    gate_up = dot(normed_mlp, gate_up_block, ((1,), (0,))).reshape(tokens, col_count, 2, -1)
    gate_vals = gate_up[:, :, 0]
    up_vals = gate_up[:, :, 1]
    sigmoid_gate = jax.nn.sigmoid(gate_vals)
    silu_gate = gate_vals * sigmoid_gate
    hidden_low = (silu_gate * up_vals).astype(low).reshape(tokens, -1)
    mlp_part = dot(hidden_low, down_block, ((1,), (0,)))
    outputs = (
        own_half(resid_mid, 1, row_index)
        + own_half(mlp_part, 1, row_index)
        + swap_row(other_half(mlp_part, 1, row_index).astype(low)).astype(jnp.float32)
    )

    cotangent_full = in_row_order(cotangent, swap_row(cotangent), row_index, 1)
    down_grad = dot(hidden_low, cotangent_full, ((0,), (0,))).astype(low)
    grad_down = scatter_out(down_grad).astype(jnp.float32)
    hidden_grad = dot(cotangent_full, down_block, ((1,), (1,))).reshape(gate_vals.shape)
    gate_grad = hidden_grad * up_vals * sigmoid_gate * (1.0 + gate_vals * (1.0 - sigmoid_gate))
    up_grad = hidden_grad * silu_gate
    gate_up_send = jnp.stack([gate_grad, up_grad], axis=2).astype(low).reshape(tokens, -1)
    mlp_back = dot(gate_up_send, gate_up_block, ((1,), (1,))).astype(low)
    normed_mlp_grad = mlp_back.astype(jnp.float32) + swap_row(mlp_back).astype(jnp.float32)
    gate_up_wgrad = dot(normed_mlp, gate_up_send, ((0,), (0,))).astype(low)
    gate_up_pieces = scatter_in(gate_up_wgrad)
    gate_wide = w_gate_up.shape[2] // 2
    grad_gate_up = jnp.stack(
        [
            return_columns(gate_up_pieces[:, :, :gate_wide], row_index),
            return_columns(gate_up_pieces[:, :, gate_wide:], row_index),
        ]
    ).astype(jnp.float32)

    mid_grad = cotangent_full.astype(jnp.float32) + norm_back(
        normed_mlp_grad, resid_mid, scale_mlp, gain_mlp
    )
    gain_mlp_grad = jnp.sum(normed_mlp_grad * resid_mid * scale_mlp, axis=0)
    mid_low = mid_grad.astype(low)
    attn_grad = dot(mid_low, out_block, ((1,), (1,))).astype(low)
    out_wgrad = dot(attn_low, mid_low, ((0,), (0,))).astype(low)
    grad_out = scatter_out(out_wgrad).astype(jnp.float32)
    query_grad, key_grad, value_grad = attention_call(
        attend_backward_kernel,
        seg_column,
        seg_line,
        (query_low, key_low, value_low, attn_grad),
        (
            jax.ShapeDtypeStruct(query_low.shape, jnp.float32),
            jax.ShapeDtypeStruct(key_low.shape, jnp.float32),
            jax.ShapeDtypeStruct(key_low.shape, jnp.float32),
        ),
        kv_count,
    )
    query_pre_grad, gain_query_grad = pull_query(query_grad.reshape(query_heads.shape))
    key_pre_grad, gain_key_grad = pull_key(key_grad.reshape(key_heads.shape))
    send = jnp.concatenate(
        [
            query_pre_grad.reshape(tokens, col_count, -1).astype(low),
            key_pre_grad.reshape(tokens, col_count, -1).astype(low),
            value_grad.reshape(tokens, col_count, -1).astype(low),
        ],
        axis=2,
    ).reshape(tokens, -1)
    in_wgrad = dot(normed_attn, send, ((0,), (0,))).astype(low)
    in_pieces = scatter_in(in_wgrad)
    grad_query = return_columns(in_pieces[:, :, :query_wide], row_index).astype(jnp.float32)
    grad_keyval = jnp.stack(
        [
            return_columns(in_pieces[:, :, query_wide : query_wide + key_wide], row_index),
            return_columns(in_pieces[:, :, query_wide + key_wide :], row_index),
        ]
    ).astype(jnp.float32)
    attn_back = dot(send, in_block, ((1,), (1,)))
    inner_part = jnp.sum(attn_back * gain_attn * resid_in, axis=-1)
    inner = (inner_part + swap_row(inner_part))[:, None]
    normed_attn_grad = own_half(attn_back, 1, row_index) + swap_row(
        other_half(attn_back, 1, row_index).astype(low)
    ).astype(jnp.float32)
    resid_own = inputs.astype(jnp.float32)
    gain_own = lax.dynamic_slice_in_dim(norm_gains, row_index * width_row, width_row)
    input_grad = (
        own_half(mid_grad, 1, row_index)
        + scale_attn * normed_attn_grad * gain_own
        - resid_own * (scale_attn * scale_attn * scale_attn) * inner / MODEL_WIDTH
    )
    gain_attn_grad = jnp.sum(normed_attn_grad * resid_own * scale_attn, axis=0)
    gain_attn_wide = lax.dynamic_update_slice_in_dim(
        jnp.zeros((MODEL_WIDTH,), jnp.float32), gain_attn_grad, row_index * width_row, 0
    )
    gains_grad = lax.psum(
        jnp.concatenate([gain_attn_wide, 0.5 * gain_mlp_grad, gain_query_grad, gain_key_grad]),
        ("dp", "row", "col"),
    )
    query_new = adam_update(
        w_query, grad_query, first_query, second_query, weight_decay, learning_rate
    )
    keyval_new = adam_update(
        keyvalue_weight,
        grad_keyval,
        keyvalue_first_moment,
        keyvalue_second_moment,
        weight_decay,
        learning_rate,
    )
    out_new = adam_update(w_out, grad_out, first_out, second_out, weight_decay, learning_rate)
    gate_up_new = adam_update(
        w_gate_up, grad_gate_up, first_gate_up, second_gate_up, weight_decay, learning_rate
    )
    down_new = adam_update(w_down, grad_down, first_down, second_down, weight_decay, learning_rate)
    gains_new = adam_update(norm_gains, gains_grad, gains_first, gains_second, 0.0, gains_rate)
    return (
        outputs,
        input_grad,
        query_new[0],
        keyval_new[0],
        out_new[0],
        gate_up_new[0],
        down_new[0],
        query_new[1],
        keyval_new[1],
        out_new[1],
        gate_up_new[1],
        down_new[1],
        query_new[2],
        keyval_new[2],
        out_new[2],
        gate_up_new[2],
        down_new[2],
        gains_new[0],
        gains_new[1],
        gains_new[2],
    )


def solution(mesh):
    in_specs = (
        P(("dp", "col"), "row"),
        P("dp", None),
        P(("dp", "col"), "row"),
        P(("row", "dp"), "col"),
        P(None, ("row", "dp"), "col"),
        P(("col", "dp"), "row"),
        P(None, ("row", "dp"), "col"),
        P(("col", "dp"), "row"),
        P(("row", "dp"), "col"),
        P(None, ("row", "dp"), "col"),
        P(("col", "dp"), "row"),
        P(None, ("row", "dp"), "col"),
        P(("col", "dp"), "row"),
        P(("row", "dp"), "col"),
        P(None, ("row", "dp"), "col"),
        P(("col", "dp"), "row"),
        P(None, ("row", "dp"), "col"),
        P(("col", "dp"), "row"),
        P(),
        P(),
        P(),
    )
    out_specs = (
        P(("dp", "col"), "row"),
        P(("dp", "col"), "row"),
        P(("row", "dp"), "col"),
        P(None, ("row", "dp"), "col"),
        P(("col", "dp"), "row"),
        P(None, ("row", "dp"), "col"),
        P(("col", "dp"), "row"),
        P(("row", "dp"), "col"),
        P(None, ("row", "dp"), "col"),
        P(("col", "dp"), "row"),
        P(None, ("row", "dp"), "col"),
        P(("col", "dp"), "row"),
        P(("row", "dp"), "col"),
        P(None, ("row", "dp"), "col"),
        P(("col", "dp"), "row"),
        P(None, ("row", "dp"), "col"),
        P(("col", "dp"), "row"),
        P(),
        P(),
        P(),
    )
    return jax.shard_map(shards, mesh=mesh, in_specs=in_specs, out_specs=out_specs, check_vma=False)
```

```python
import jax
import jax.numpy as jnp
from jax import lax
from jax.experimental import pallas as pl
from jax.experimental.pallas import tpu as pltpu
from jax.sharding import PartitionSpec as P

MODEL_WIDTH = 1024
HEAD_SIZE = 128
STEP = 10


epsilon = 1e-06
rope_base = 1000000.0
masked_score = -1e30
beta_first = 0.9
beta_second = 0.999
learning_rate = 0.05
gains_rate = 0.6
adam_epsilon = 1e-08
weight_decay = 0.1
score_scale = HEAD_SIZE ** (-0.5)


def rms_scale(values):
    return lax.rsqrt(jnp.mean(values * values, axis=-1, keepdims=True) + epsilon)


def rotate(values, cosine_table, sinus_table):
    half_width = values.shape[-1] // 2
    turned = jnp.concatenate([-values[..., half_width:], values[..., :half_width]], axis=-1)
    return values * cosine_table + turned * sinus_table


def rope_tables(positions):
    exponent = jnp.arange(HEAD_SIZE // 2, dtype=jnp.float32) * (2.0 / HEAD_SIZE)
    inverse = jnp.exp(-jnp.log(jnp.float32(rope_base)) * exponent)
    angles = positions.astype(jnp.float32)[..., None] * inverse
    angles = jnp.concatenate([angles, angles], axis=-1)
    return (jnp.cos(angles), jnp.sin(angles))


def allowed(segment_ids):
    length = segment_ids.shape[-1]
    order = jnp.arange(length)
    causal = order[None, :] <= order[:, None]
    return (segment_ids[..., :, None] == segment_ids[..., None, :]) & causal


def head_slice_part(pre_values, gain_vec, cosine_table, sinus_table):
    return rotate(pre_values * rms_scale(pre_values) * gain_vec, cosine_table, sinus_table)


def swap_row(values):
    return lax.ppermute(values, "row", [(0, 1), (1, 0)])


def own_half(values, axis, row_index):
    width = values.shape[axis] // 2
    return lax.dynamic_slice_in_dim(values, row_index * width, width, axis)


def other_half(values, axis, row_index):
    width = values.shape[axis] // 2
    return lax.dynamic_slice_in_dim(values, (1 - row_index) * width, width, axis)


def in_row_order(own, peer, row_index, axis):
    return jnp.where(
        row_index == 0,
        jnp.concatenate([own, peer], axis=axis),
        jnp.concatenate([peer, own], axis=axis),
    )


def exchange_columns(block, row_index):
    peer = swap_row(other_half(block, 1, row_index))
    return in_row_order(own_half(block, 1, row_index)[None], peer[None], row_index, 0)


def return_columns(pieces, row_index):
    own = lax.dynamic_index_in_dim(pieces, row_index, 0, keepdims=False)
    peer = swap_row(lax.dynamic_index_in_dim(pieces, 1 - row_index, 0, keepdims=False))
    return in_row_order(own, peer, row_index, 1)


def block_moves(dp_count):
    half = dp_count // 2
    moves = []
    for row in range(2):
        for place in range(dp_count):
            target = 2 * (2 * (place % half) + row) + place // half
            moves.append((2 * place + row, target))
    return moves


def gather_in(pieces):
    dp_count, col_count = lax.axis_size("dp"), lax.axis_size("col")
    gathered = lax.all_gather(pieces, ("dp", "col"), axis=0, tiled=False)
    rows, columns = pieces.shape[1:]
    gathered = gathered.reshape(dp_count, col_count, 2, rows, columns)
    return gathered.transpose(2, 0, 3, 1, 4).reshape(2 * dp_count * rows, col_count * columns)


def scatter_in(grad):
    dp_count, col_count = lax.axis_size("dp"), lax.axis_size("col")
    rows, columns = grad.shape[0] // (2 * dp_count), grad.shape[1] // col_count
    pieces = grad.reshape(2, dp_count, rows, col_count, columns).transpose(1, 3, 0, 2, 4)
    pieces = pieces.reshape(dp_count * col_count, 2, rows, columns)
    return lax.psum_scatter(pieces, ("dp", "col"), scatter_dimension=0, tiled=False)


def gather_out(shard):
    dp_count, col_count = lax.axis_size("dp"), lax.axis_size("col")
    moved = lax.ppermute(shard, ("dp", "row"), block_moves(dp_count))
    gathered = lax.all_gather(moved, ("dp", "col"), axis=0, tiled=False)
    rows, columns = shard.shape
    gathered = gathered.reshape(dp_count // 2, 2, col_count, rows, columns)
    return gathered.transpose(2, 0, 3, 1, 4).reshape(
        col_count * (dp_count // 2) * rows, 2 * columns
    )


def scatter_out(grad):
    dp_count, col_count = lax.axis_size("dp"), lax.axis_size("col")
    rows, columns = grad.shape[0] // (col_count * (dp_count // 2)), grad.shape[1] // 2
    pieces = grad.reshape(col_count, dp_count // 2, rows, 2, columns).transpose(1, 3, 0, 2, 4)
    pieces = pieces.reshape(dp_count * col_count, rows, columns)
    own = lax.psum_scatter(pieces, ("dp", "col"), scatter_dimension=0, tiled=False)
    back = [(target, source) for source, target in block_moves(dp_count)]
    return lax.ppermute(own, ("dp", "row"), back)


def dot(left, right, contract):
    return lax.dot_general(
        left, right, ((contract[0], contract[1]), ((), ())), preferred_element_type=jnp.float32
    )


def probabilities(query, keys, permitted):
    scores = dot(query, keys, ((1,), (1,))) * score_scale
    scores = jnp.where(permitted, scores, masked_score)
    exp_scores = jnp.exp(scores - jnp.max(scores, axis=-1, keepdims=True))
    return exp_scores / jnp.sum(exp_scores, axis=-1, keepdims=True)


def permitted_of(seg_column, seg_line):
    length = seg_line.shape[1]
    place = lax.broadcasted_iota(jnp.int32, (length, length), 0)
    other = lax.broadcasted_iota(jnp.int32, (length, length), 1)
    return (seg_column[...] == seg_line[...]) & (other <= place)


def attend_forward_kernel(seg_column, seg_line, query, keys, values, mixed):
    permitted = permitted_of(seg_column, seg_line)
    for head in range(query.shape[1] // HEAD_SIZE):
        columns = slice(head * HEAD_SIZE, (head + 1) * HEAD_SIZE)
        probs = probabilities(query[:, columns], keys[...], permitted)
        mixed[:, columns] = dot(
            probs.astype(jnp.bfloat16), values[...], ((1,), (0,))
        ).astype(jnp.bfloat16)


def attend_backward_kernel(
    seg_column, seg_line, query, keys, values, grad, query_grad, key_grad, value_grad
):
    permitted = permitted_of(seg_column, seg_line)
    key_total, value_total = None, None
    for head in range(query.shape[1] // HEAD_SIZE):
        columns = slice(head * HEAD_SIZE, (head + 1) * HEAD_SIZE)
        probs = probabilities(query[:, columns], keys[...], permitted)
        prob_grad = dot(grad[:, columns], values[...], ((1,), (1,)))
        inner = jnp.sum(probs * prob_grad, axis=-1, keepdims=True)
        score_low = (probs * (prob_grad - inner)).astype(jnp.bfloat16)
        query_grad[:, columns] = dot(score_low, keys[...], ((1,), (0,))) * score_scale
        key_part = dot(score_low, query[:, columns], ((0,), (0,)))
        value_part = dot(probs.astype(jnp.bfloat16), grad[:, columns], ((0,), (0,)))
        key_total = key_part if head == 0 else key_total + key_part
        value_total = value_part if head == 0 else value_total + value_part
    key_grad[...] = key_total * score_scale
    value_grad[...] = value_total


def attention_call(kernel, seg_column, seg_line, arrays, outs, kv_count):
    length = seg_column.shape[0]

    def block(array):
        return pl.BlockSpec((length, array.shape[1] // kv_count), lambda head: (0, head))

    return pl.pallas_call(
        kernel,
        grid=(kv_count,),
        in_specs=[
            pl.BlockSpec(seg_column.shape, lambda head: (0, 0)),
            pl.BlockSpec(seg_line.shape, lambda head: (0, 0)),
        ]
        + [block(array) for array in arrays],
        out_specs=[block(out) for out in outs],
        out_shape=list(outs),
        compiler_params=pltpu.CompilerParams(vmem_limit_bytes=48 * 1024 * 1024),
    )(seg_column, seg_line, *arrays)


def norm_back(grad_normed, resid, scale, gain_vec):
    weighted = grad_normed * gain_vec
    inner = jnp.sum(weighted * resid, axis=-1, keepdims=True)
    resid_grad = scale * weighted - resid * (scale * scale * scale) * inner / MODEL_WIDTH
    return resid_grad


def adam_update(weight, gradient, first, second, decay, rate):
    first_new = beta_first * first + (1.0 - beta_first) * gradient
    second_new = beta_second * second + (1.0 - beta_second) * gradient * gradient
    first_hat = first_new / (1.0 - beta_first**STEP)
    second_hat = second_new / (1.0 - beta_second**STEP)
    weight_new = weight - rate * (
        first_hat / (jnp.sqrt(second_hat) + adam_epsilon) + decay * weight
    )
    return (weight_new, first_new, second_new)


def shards(
    inputs,
    segments,
    cotangent,
    w_query,
    keyvalue_weight,
    w_out,
    w_gate_up,
    w_down,
    first_query,
    keyvalue_first_moment,
    first_out,
    first_gate_up,
    first_down,
    second_query,
    keyvalue_second_moment,
    second_out,
    second_gate_up,
    second_down,
    norm_gains,
    gains_first,
    gains_second,
):
    low = jnp.bfloat16
    row_index = lax.axis_index("row")
    tokens = inputs.shape[0]
    width_row = inputs.shape[1]

    query_key_value = jnp.concatenate(
        [
            exchange_columns(block.astype(low), row_index)
            for block in (w_query, keyvalue_weight[0], keyvalue_weight[1])
        ],
        axis=2,
    )
    in_block = gather_in(query_key_value)
    out_block = gather_out(w_out.astype(low))
    gate_up_block = gather_in(
        jnp.concatenate(
            [exchange_columns(w_gate_up[which].astype(low), row_index) for which in (0, 1)],
            axis=2,
        )
    )
    down_block = gather_out(w_down.astype(low))

    gain_attn = norm_gains[:MODEL_WIDTH]
    gain_mlp = norm_gains[MODEL_WIDTH : 2 * MODEL_WIDTH]
    gain_query = norm_gains[2 * MODEL_WIDTH : 2 * MODEL_WIDTH + HEAD_SIZE]
    key_norm_gain = norm_gains[2 * MODEL_WIDTH + HEAD_SIZE :]
    segment = lax.dynamic_index_in_dim(segments, lax.axis_index("col"), 0, keepdims=False)
    seg_column, seg_line = segment[:, None], segment[None, :]
    positions = jnp.sum(allowed(segment).astype(jnp.int32), axis=-1) - 1
    cosine_table, sinus_table = rope_tables(positions)
    cosine_table = cosine_table[:, None, :]
    sinus_table = sinus_table[:, None, :]

    resid_in = in_row_order(inputs, swap_row(inputs), row_index, 1).astype(jnp.float32)
    scale_attn = rms_scale(resid_in)
    normed_attn = (resid_in * scale_attn * gain_attn).astype(low)
    col_count = lax.axis_size("col")
    query_wide = w_query.shape[1] // 2
    key_wide = keyvalue_weight.shape[2] // 2
    projected = dot(normed_attn, in_block, ((1,), (0,))).reshape(tokens, col_count, -1)
    query_heads = projected[:, :, :query_wide].reshape(tokens, -1, HEAD_SIZE)
    key_heads = projected[:, :, query_wide : query_wide + key_wide].reshape(tokens, -1, HEAD_SIZE)
    value_low = projected[:, :, query_wide + key_wide :].reshape(tokens, -1).astype(low)
    kv_count = key_heads.shape[1]

    def normed_heads(pre_values, gain_vec):
        return head_slice_part(pre_values, gain_vec, cosine_table, sinus_table)

    query_rot, pull_query = jax.vjp(normed_heads, query_heads, gain_query)
    key_rot, pull_key = jax.vjp(normed_heads, key_heads, key_norm_gain)
    query_low = query_rot.astype(low).reshape(tokens, -1)
    key_low = key_rot.astype(low).reshape(tokens, -1)
    (attn_low,) = attention_call(
        attend_forward_kernel,
        seg_column,
        seg_line,
        (query_low, key_low, value_low),
        (jax.ShapeDtypeStruct(query_low.shape, low),),
        kv_count,
    )
    attn_part = dot(attn_low, out_block, ((1,), (0,))).astype(low)
    attn_sum = attn_part.astype(jnp.float32) + swap_row(attn_part).astype(jnp.float32)
    resid_mid = resid_in + attn_sum
    scale_mlp = rms_scale(resid_mid)
    normed_mlp = (resid_mid * scale_mlp * gain_mlp).astype(low)
    gate_up = dot(normed_mlp, gate_up_block, ((1,), (0,))).reshape(tokens, col_count, 2, -1)
    gate_vals = gate_up[:, :, 0]
    up_vals = gate_up[:, :, 1]
    sigmoid_gate = jax.nn.sigmoid(gate_vals)
    silu_gate = gate_vals * sigmoid_gate
    hidden_low = (silu_gate * up_vals).astype(low).reshape(tokens, -1)
    mlp_part = dot(hidden_low, down_block, ((1,), (0,)))
    outputs = (
        own_half(resid_mid, 1, row_index)
        + own_half(mlp_part, 1, row_index)
        + swap_row(other_half(mlp_part, 1, row_index).astype(low)).astype(jnp.float32)
    )

    cotangent_full = in_row_order(cotangent, swap_row(cotangent), row_index, 1)
    hidden_kept, _ = lax.optimization_barrier((hidden_low, down_block))
    down_grad = dot(hidden_kept, cotangent_full, ((0,), (0,))).astype(low)
    grad_down = scatter_out(down_grad).astype(jnp.float32)
    hidden_grad = dot(cotangent_full, down_block, ((1,), (1,))).reshape(gate_vals.shape)
    gate_grad = hidden_grad * up_vals * sigmoid_gate * (1.0 + gate_vals * (1.0 - sigmoid_gate))
    up_grad = hidden_grad * silu_gate
    gate_up_send = jnp.stack([gate_grad, up_grad], axis=2).astype(low).reshape(tokens, -1)
    mlp_back = dot(gate_up_send, gate_up_block, ((1,), (1,))).astype(low)
    normed_mlp_grad = mlp_back.astype(jnp.float32) + swap_row(mlp_back).astype(jnp.float32)
    gate_up_wgrad = dot(normed_mlp, gate_up_send, ((0,), (0,))).astype(low)
    gate_up_pieces = scatter_in(gate_up_wgrad)
    gate_wide = w_gate_up.shape[2] // 2
    grad_gate_up = jnp.stack(
        [
            return_columns(gate_up_pieces[:, :, :gate_wide], row_index),
            return_columns(gate_up_pieces[:, :, gate_wide:], row_index),
        ]
    ).astype(jnp.float32)

    mid_grad = cotangent_full.astype(jnp.float32) + norm_back(
        normed_mlp_grad, resid_mid, scale_mlp, gain_mlp
    )
    gain_mlp_grad = jnp.sum(normed_mlp_grad * resid_mid * scale_mlp, axis=0)
    mid_low = mid_grad.astype(low)
    attn_grad = dot(mid_low, out_block, ((1,), (1,))).astype(low)
    out_wgrad = dot(attn_low, mid_low, ((0,), (0,))).astype(low)
    grad_out = scatter_out(out_wgrad).astype(jnp.float32)
    query_grad, key_grad, value_grad = attention_call(
        attend_backward_kernel,
        seg_column,
        seg_line,
        (query_low, key_low, value_low, attn_grad),
        (
            jax.ShapeDtypeStruct(query_low.shape, jnp.float32),
            jax.ShapeDtypeStruct(key_low.shape, jnp.float32),
            jax.ShapeDtypeStruct(key_low.shape, jnp.float32),
        ),
        kv_count,
    )
    query_pre_grad, gain_query_grad = pull_query(query_grad.reshape(query_heads.shape))
    key_pre_grad, gain_key_grad = pull_key(key_grad.reshape(key_heads.shape))
    send = jnp.concatenate(
        [
            query_pre_grad.reshape(tokens, col_count, -1).astype(low),
            key_pre_grad.reshape(tokens, col_count, -1).astype(low),
            value_grad.reshape(tokens, col_count, -1).astype(low),
        ],
        axis=2,
    ).reshape(tokens, -1)
    in_wgrad = dot(normed_attn, send, ((0,), (0,))).astype(low)
    in_pieces = scatter_in(in_wgrad)
    grad_query = return_columns(in_pieces[:, :, :query_wide], row_index).astype(jnp.float32)
    grad_keyval = jnp.stack(
        [
            return_columns(in_pieces[:, :, query_wide : query_wide + key_wide], row_index),
            return_columns(in_pieces[:, :, query_wide + key_wide :], row_index),
        ]
    ).astype(jnp.float32)
    attn_back = dot(send, in_block, ((1,), (1,)))
    inner_part = jnp.sum(attn_back * gain_attn * resid_in, axis=-1)
    inner = (inner_part + swap_row(inner_part))[:, None]
    normed_attn_grad = own_half(attn_back, 1, row_index) + swap_row(
        other_half(attn_back, 1, row_index).astype(low)
    ).astype(jnp.float32)
    resid_own = inputs.astype(jnp.float32)
    gain_own = lax.dynamic_slice_in_dim(norm_gains, row_index * width_row, width_row)
    input_grad = (
        own_half(mid_grad, 1, row_index)
        + scale_attn * normed_attn_grad * gain_own
        - resid_own * (scale_attn * scale_attn * scale_attn) * inner / MODEL_WIDTH
    )
    gain_attn_grad = jnp.sum(normed_attn_grad * resid_own * scale_attn, axis=0)
    gain_attn_wide = lax.dynamic_update_slice_in_dim(
        jnp.zeros((MODEL_WIDTH,), jnp.float32), gain_attn_grad, row_index * width_row, 0
    )
    gains_grad = lax.psum(
        jnp.concatenate([gain_attn_wide, 0.5 * gain_mlp_grad, gain_query_grad, gain_key_grad]),
        ("dp", "row", "col"),
    )
    query_new = adam_update(
        w_query, grad_query, first_query, second_query, weight_decay, learning_rate
    )
    keyval_new = adam_update(
        keyvalue_weight,
        grad_keyval,
        keyvalue_first_moment,
        keyvalue_second_moment,
        weight_decay,
        learning_rate,
    )
    out_new = adam_update(w_out, grad_out, first_out, second_out, weight_decay, learning_rate)
    gate_up_new = adam_update(
        w_gate_up, grad_gate_up, first_gate_up, second_gate_up, weight_decay, learning_rate
    )
    down_new = adam_update(w_down, grad_down, first_down, second_down, weight_decay, learning_rate)
    gains_new = adam_update(norm_gains, gains_grad, gains_first, gains_second, 0.0, gains_rate)
    return (
        outputs,
        input_grad,
        query_new[0],
        keyval_new[0],
        out_new[0],
        gate_up_new[0],
        down_new[0],
        query_new[1],
        keyval_new[1],
        out_new[1],
        gate_up_new[1],
        down_new[1],
        query_new[2],
        keyval_new[2],
        out_new[2],
        gate_up_new[2],
        down_new[2],
        gains_new[0],
        gains_new[1],
        gains_new[2],
    )


def solution(mesh):
    in_specs = (
        P(("dp", "col"), "row"),
        P("dp", None),
        P(("dp", "col"), "row"),
        P(("row", "dp"), "col"),
        P(None, ("row", "dp"), "col"),
        P(("col", "dp"), "row"),
        P(None, ("row", "dp"), "col"),
        P(("col", "dp"), "row"),
        P(("row", "dp"), "col"),
        P(None, ("row", "dp"), "col"),
        P(("col", "dp"), "row"),
        P(None, ("row", "dp"), "col"),
        P(("col", "dp"), "row"),
        P(("row", "dp"), "col"),
        P(None, ("row", "dp"), "col"),
        P(("col", "dp"), "row"),
        P(None, ("row", "dp"), "col"),
        P(("col", "dp"), "row"),
        P(),
        P(),
        P(),
    )
    out_specs = (
        P(("dp", "col"), "row"),
        P(("dp", "col"), "row"),
        P(("row", "dp"), "col"),
        P(None, ("row", "dp"), "col"),
        P(("col", "dp"), "row"),
        P(None, ("row", "dp"), "col"),
        P(("col", "dp"), "row"),
        P(("row", "dp"), "col"),
        P(None, ("row", "dp"), "col"),
        P(("col", "dp"), "row"),
        P(None, ("row", "dp"), "col"),
        P(("col", "dp"), "row"),
        P(("row", "dp"), "col"),
        P(None, ("row", "dp"), "col"),
        P(("col", "dp"), "row"),
        P(None, ("row", "dp"), "col"),
        P(("col", "dp"), "row"),
        P(),
        P(),
        P(),
    )
    return jax.shard_map(shards, mesh=mesh, in_specs=in_specs, out_specs=out_specs, check_vma=False)
```
